1024 devices in a mesh: row: 128 (over y, x, core), col: 8 (over z).
Axes of the slice: x: 8, y: 8, z: 8, core: 2. Of those that a mesh axis runs over, the one named last changes fastest.
Arguments:
- features: bfloat16 [8, 128, 16, 512], P('col', 'row'), may hold values from -6 to 6
- weight: bfloat16 [512, 512], replicated, may hold values from -0.25 to 0.25
- cotangent: bfloat16 [128, 8, 16, 512], P('row', 'col'), may hold values from -6 to 6
- tile_mask: int32 [128, 8, 12, 128, 128], P('row', 'col'), may hold values 0 or 1
- tile_cols: int32 [128, 8, 12], P('row', 'col'), may hold values from 0 to 15, as said below
- tile_count: int32 [128, 8], P('row', 'col'), may hold values from 3 to 12, as said below
- degree: int32 [128, 128], P('row'), may hold values from 384 to 3073
Outputs:
- activated: bfloat16 [128, 8, 16, 512], P('row', 'col')
- feature_grad: bfloat16 [8, 128, 16, 512], P('col', 'row')
- weight_grad: float32 [512, 512], P('col')
The draws below stay inside these ranges and needn't reach their ends.
Inputs may be any that keep to these rules, and one draw needn't show every extreme that they name: `tile_cols`: within one block the 12 tile columns are distinct. Only the first tile_count[r, c] slots of a block are live; in every draw some whole row of blocks has all 12 slots live.
All inputs are finite; a program needn't handle non-finite values. No bound on the sum of `tile_mask` on one device may be relied on, other than what follows from the above.
Results may differ from the reference program's by a relative error of at most 0.007.
Values may be sent and summed in bfloat16 or wider, within the bound.
No kernel may reach another device: no remote copies, remote signals or barrier semaphores. Data moves between devices by JAX's collectives and lax.ppermute only.
A program may use at most 32 MiB of HBM per device.

```python
import jax
import jax.numpy as jnp
from jax import lax

WIDTH = 512
NODES_DEV = 16
TILE = 128
GRID_ROWS = 128
GRID_COLS = 8
BLOCK_ROWS = 128
COL_NODES = 2048
NODES = 16384
PANELS = 16
K_TILES = 12
N_COL = 8


def draw_tile_cols(key, part):
    scores = jax.random.randint(key, (GRID_ROWS, GRID_COLS, PANELS), 0, 1 << 20) * PANELS
    scores = scores + jnp.arange(PANELS, dtype=jnp.int32)[None, None, :]
    order = jnp.argsort(scores, axis=-1)
    return order[:, :, :K_TILES].astype(jnp.int32)


def draw_tile_count(key, part):
    counts = jax.random.randint(key, (GRID_ROWS, GRID_COLS), max(K_TILES // 4, 1), K_TILES + 1)
    full_row = jax.random.randint(jax.random.fold_in(key, 7), (), 0, GRID_ROWS)
    row_ids = jnp.arange(GRID_ROWS, dtype=jnp.int32)[:, None]
    return jnp.where(row_ids == full_row, K_TILES, counts).astype(jnp.int32)


def with_ends(entries, own_key, least, high):
    extent = entries.shape
    place = [jax.random.randint(jax.random.fold_in(own_key, axis), (), 0, extent[axis]) for axis in range(len(extent))]
    entries = entries.at[tuple(place)].set(least)
    longest = extent.index(max(extent))
    place[longest] = (place[longest] + 1) % extent[longest]
    return entries.at[tuple(place)].set(high)


def strengthened(result, stream_key, source, target, blocks, factor):
    def block_of(dim):
        return (jnp.arange(result.shape[dim]) // (result.shape[dim] // blocks)).reshape((-1,) + (1,) * (result.ndim - 1 - dim))

    first = jax.random.permutation(stream_key, blocks)[block_of(target)]
    second = (block_of(target) + blocks // 2) % blocks
    return jnp.where((block_of(source) == first) | (block_of(source) == second), factor * result, result)


def block_levels(own_key, extent, cuts, least, high):
    gain, own = 1.0, jax.random.fold_in(own_key, 6)
    for dim, shards_of in cuts:
        draws = jnp.exp(jax.random.uniform(jax.random.fold_in(own, dim), (shards_of,), jnp.float32, least / len(cuts), high / len(cuts)))
        gain = gain * jnp.repeat(draws, extent[dim] // shards_of).reshape([-1 if axis == dim else 1 for axis in range(len(extent))])
    return gain


def gaussian(key, shape, width, reach, shards=(), kind=jnp.bfloat16):
    entries = width * jax.random.normal(key, shape, jnp.float32)
    if shards:
        entries = entries * block_levels(key, shape, shards, -0.22, 0.18)
    return jnp.clip(entries, -reach, reach).astype(kind)


def noise_with(stream_key, dims, width, reach, shards, heavy, kind=jnp.bfloat16):
    entries = width * jax.random.normal(stream_key, dims, jnp.float32)
    if shards:
        entries = entries * block_levels(stream_key, dims, shards, -0.22, 0.18)
    return jnp.clip(strengthened(entries, jax.random.fold_in(stream_key, 3), *heavy), -reach, reach).astype(kind)


def setup_inputs(seed: int = 0) -> dict:
    streams_of = jax.random.split(jax.random.key(seed), 8)
    return {
        "features": gaussian(streams_of[0], (GRID_COLS, GRID_ROWS, NODES_DEV, WIDTH), 1.0, 6.0, ((0, 8), (1, 128))),
        "weight": gaussian(streams_of[1], (WIDTH, WIDTH), WIDTH ** -0.5, 0.25),
        "cotangent": noise_with(streams_of[2], (GRID_ROWS, GRID_COLS, NODES_DEV, WIDTH), 1.0, 6.0, ((0, 128), (1, 8)), (0, 1, 8, 2.0)),
        "tile_mask": with_ends((jax.random.randint(streams_of[3], (GRID_ROWS, GRID_COLS, K_TILES, BLOCK_ROWS, TILE), 0, 8) < 1).astype(jnp.int32), jax.random.fold_in(streams_of[3], 1), 0, 1),
        "tile_cols": draw_tile_cols(jax.random.fold_in(streams_of[7], 71), 0),
        "tile_count": draw_tile_count(jax.random.fold_in(streams_of[7], 71), 0),
        "degree": with_ends(jax.random.randint(streams_of[6], (GRID_ROWS, BLOCK_ROWS), max(1, N_COL * K_TILES * TILE // 32), N_COL * K_TILES * TILE // 4 + 2), jax.random.fold_in(streams_of[6], 1), max(1, N_COL * K_TILES * TILE // 32), (N_COL * K_TILES * TILE // 4 + 2) - 1).astype(jnp.int32),
    }


def block_weights(mask_row, cols_row, count_row, degree_row):
    live_tiles = (jnp.arange(K_TILES, dtype=jnp.int32)[None, :] < count_row[:, None]).astype(jnp.float32)
    onehot = (cols_row[:, :, None] == jnp.arange(PANELS, dtype=jnp.int32)[None, None, :]).astype(jnp.float32)
    onehot = onehot * live_tiles[:, :, None]
    counts = jnp.einsum('ckp,ckit->cipt', onehot, mask_row.astype(jnp.float32))
    counts = counts.reshape(GRID_COLS, BLOCK_ROWS, COL_NODES)
    row_scale = lax.rsqrt(degree_row.astype(jnp.float32))
    return (counts * row_scale[None, :, None]).astype(jnp.bfloat16)

def reference(features, weight, cotangent, tile_mask, tile_cols, tile_count, degree):
    panels = features.reshape(GRID_COLS, COL_NODES, WIDTH).astype(jnp.float32)

    def forward_row(row_items):
        weights_row = block_weights(*row_items)
        return jnp.einsum('cij,cjf->if', weights_row.astype(jnp.float32), panels)
    aggregate = lax.map(forward_row, (tile_mask, tile_cols, tile_count, degree))
    node_inputs = aggregate.reshape(NODES, WIDTH).astype(jnp.bfloat16)
    preact = jnp.dot(node_inputs, weight, preferred_element_type=jnp.float32)
    activated = jax.nn.silu(preact).astype(jnp.bfloat16)
    sigma = jax.nn.sigmoid(preact)
    slope = sigma * (1.0 + preact * (1.0 - sigma))
    slope_grad = (cotangent.reshape(NODES, WIDTH).astype(jnp.float32) * slope).astype(jnp.bfloat16)
    weight_grad = jnp.dot(node_inputs.T, slope_grad, preferred_element_type=jnp.float32)
    projected = jnp.dot(slope_grad, weight.T, preferred_element_type=jnp.float32).astype(jnp.bfloat16)
    projected = projected.reshape(GRID_ROWS, BLOCK_ROWS, WIDTH)

    def backward_row(running, row_items):
        mask_row, cols_row, count_row, degree_row, projected_row = row_items
        weights_row = block_weights(mask_row, cols_row, count_row, degree_row)
        update = jnp.einsum('cij,if->cjf', weights_row.astype(jnp.float32), projected_row.astype(jnp.float32))
        return (running + update, None)
    start_sum = jnp.zeros((GRID_COLS, COL_NODES, WIDTH), jnp.float32)
    feature_sum, unused = lax.scan(backward_row, start_sum, (tile_mask, tile_cols, tile_count, degree, projected))
    feature_grad = feature_sum.astype(jnp.bfloat16).reshape(GRID_COLS, GRID_ROWS, NODES_DEV, WIDTH)
    activated = activated.reshape(GRID_ROWS, GRID_COLS, NODES_DEV, WIDTH)
    return (activated, feature_grad, weight_grad)
```

```python
import jax
import jax.numpy as jnp
from jax import lax
from jax.sharding import Mesh, PartitionSpec as P

ROW = ("y", "xh", "xl", "core")
CHIPS = ("y", "xh", "xl")
GROUP = ("xl", "core")
TEAM = ("xl", "core", "z")
SWAP = [(0, 1), (1, 0)]
MEMBERS = 4


def slope_of(preact):
    sigma = jax.nn.sigmoid(preact)
    return sigma * (1.0 + preact * (1.0 - sigma))


def exclusive(blocks):
    core = lax.axis_index("core") == 1
    half = lax.axis_index("xl") == 1
    a, b, c, d = (blocks[i] for i in range(MEMBERS))
    a, b, c, d = (
        jnp.where(core, b, a),
        jnp.where(core, a, b),
        jnp.where(core, d, c),
        jnp.where(core, c, d),
    )
    return [
        jnp.where(half, c, a),
        jnp.where(half, d, b),
        jnp.where(half, a, c),
        jnp.where(half, b, d),
    ]


def dense_of(tile_mask, tile_cols, tile_count, degree, panel_count):
    slots, block_rows, tile_width = tile_mask.shape
    live = (jnp.arange(slots, dtype=jnp.int32) < tile_count).astype(jnp.float32)
    onehot = (tile_cols[:, None] == jnp.arange(panel_count, dtype=jnp.int32)[None, :]).astype(
        jnp.float32
    )
    onehot = onehot * live[:, None]
    counts = jnp.einsum("kp,kit->ipt", onehot, tile_mask.astype(jnp.float32))
    counts = counts.reshape(block_rows, panel_count * tile_width)
    return (counts * lax.rsqrt(degree.astype(jnp.float32))[:, None]).astype(jnp.bfloat16)


def body(features, weight, cotangent, tile_mask, tile_cols, tile_count, degree):
    f32, bf16 = jnp.float32, jnp.bfloat16
    node_rows, width = features.shape[2], features.shape[3]
    rows = lax.axis_size(ROW)
    depth = lax.axis_size("z")
    chips = lax.axis_size(CHIPS)
    part = width // MEMBERS
    col_nodes = rows * node_rows
    block_rows = tile_mask.shape[3]

    own = features[0, 0].reshape(node_rows, MEMBERS, part).transpose(1, 0, 2)
    send = jnp.broadcast_to(own[None], (rows // MEMBERS, MEMBERS, node_rows, part))
    panels = lax.all_to_all(send.reshape(rows, node_rows, part), ROW, 0, 0)
    panels = panels.reshape(col_nodes, part)

    dense = dense_of(
        tile_mask[0, 0], tile_cols[0, 0], tile_count[0, 0], degree[0], col_nodes // tile_mask.shape[4]
    )
    across = lax.ppermute(dense, "xl", SWAP)
    blocks = [dense, lax.ppermute(dense, "core", SWAP), across, lax.ppermute(across, "core", SWAP)]

    partial = [jnp.dot(b, panels, preferred_element_type=f32).astype(bf16) for b in blocks]
    partial = jnp.stack(exclusive(partial)).reshape(MEMBERS * depth, node_rows, part)
    sums = lax.all_to_all(partial, TEAM, 0, 0).reshape(MEMBERS, depth, node_rows, part)
    sums = jnp.sum(sums.astype(f32), axis=1)
    own_inputs = jnp.concatenate([sums[m] for m in range(MEMBERS)], axis=1).astype(bf16)

    own_pre = jnp.dot(own_inputs, weight, preferred_element_type=f32)
    activated = jax.nn.silu(own_pre).astype(bf16)
    own_slope = (cotangent[0, 0].astype(f32) * slope_of(own_pre)).astype(bf16)
    own_proj = lax.dot_general(
        own_slope, weight, (((1,), (1,)), ((), ())), preferred_element_type=f32
    ).astype(bf16)

    lanes = 128
    share = width // depth
    per_lane = lanes // share
    quarters = jnp.stack(
        [
            jnp.concatenate(
                [own_proj[:, m * part : (m + 1) * part], own_slope[:, m * part : (m + 1) * part]], axis=1
            )
            for m in range(MEMBERS)
        ]
    )
    slices = jnp.stack(
        [own_inputs[:, (d // per_lane) * lanes : (d // per_lane + 1) * lanes] for d in range(depth)]
    )
    both = jnp.concatenate(
        [
            jnp.broadcast_to(quarters[:, None], (MEMBERS, depth, node_rows, 2 * part)),
            jnp.broadcast_to(slices[None], (MEMBERS, depth, node_rows, lanes)),
        ],
        axis=3,
    ).reshape(MEMBERS * depth, node_rows, 2 * part + lanes)
    both = lax.all_to_all(both, TEAM, 0, 0).reshape(MEMBERS * block_rows, 2 * part + lanes)
    proj = exclusive(both[:, :part].reshape(MEMBERS, block_rows, part))
    contract_rows = (((0,), (0,)), ((), ()))
    grad = sum(
        lax.dot_general(b, p, contract_rows, preferred_element_type=f32)
        for b, p in zip(blocks, proj, strict=True)
    )
    grad = grad.astype(bf16).reshape(rows, node_rows, part)
    term = lax.dot_general(
        both[:, 2 * part :], both[:, part : 2 * part], contract_rows, preferred_element_type=f32
    )
    term = term.reshape(per_lane, share, part)
    term = lax.dynamic_index_in_dim(term, lax.axis_index("z") % per_lane, 0, keepdims=False)
    extra = 8
    term = jnp.broadcast_to(
        term.astype(bf16)[:, None, None, :], (chips, rows // chips, extra, part)
    ).reshape(rows, extra, part)
    out = lax.all_to_all(jnp.concatenate([grad, term], axis=1), ROW, 0, 0)
    out = out.reshape(rows // MEMBERS, MEMBERS, node_rows + extra, part)
    total = jnp.sum(out[:, :, :node_rows].astype(f32), axis=0)
    feature_grad = jnp.concatenate([total[m] for m in range(MEMBERS)], axis=1).astype(bf16)
    weight_row = jnp.sum(out[:, :, node_rows].astype(f32), axis=0).reshape(1, 1, width)
    weight_grad = lax.all_to_all(jnp.broadcast_to(weight_row, (chips, 1, width)), CHIPS, 0, 0)
    return (
        activated.reshape(1, 1, node_rows, width),
        feature_grad.reshape(1, 1, node_rows, width),
        weight_grad.reshape(chips, width),
    )


def solution(mesh):
    fine = Mesh(mesh.devices.reshape(8, 4, 2, 2, 8), ("y", "xh", "xl", "core", "z"))
    in_specs = (
        P("z", ROW, None, None),
        P(),
        P(ROW, "z", None, None),
        P(ROW, "z", None, None, None),
        P(ROW, "z", None),
        P(ROW, "z"),
        P(ROW, None),
    )
    out_specs = (P(ROW, "z", None, None), P("z", ROW, None, None), P("z", None))
    return jax.shard_map(body, mesh=fine, in_specs=in_specs, out_specs=out_specs, check_vma=False)
```

```python
import jax
import jax.numpy as jnp
from jax import lax
from jax.sharding import Mesh, PartitionSpec as P

ROW = ("yh", "yl", "xh", "xl", "core")
CUBE = ("yl", "xl", "core")
TEAM = ("xl", "core", "z")
SWAP = [(0, 1), (1, 0)]
MEMBERS = 4


def slope_of(preact):
    sigma = jax.nn.sigmoid(preact)
    return sigma * (1.0 + preact * (1.0 - sigma))


def exclusive(blocks):
    core = lax.axis_index("core") == 1
    half = lax.axis_index("xl") == 1
    a, b, c, d = (blocks[i] for i in range(MEMBERS))
    a, b, c, d = (
        jnp.where(core, b, a),
        jnp.where(core, a, b),
        jnp.where(core, d, c),
        jnp.where(core, c, d),
    )
    return [
        jnp.where(half, c, a),
        jnp.where(half, d, b),
        jnp.where(half, a, c),
        jnp.where(half, b, d),
    ]


def dense_of(tile_mask, tile_cols, tile_count, degree, panel_count):
    slots, block_rows, tile_width = tile_mask.shape
    live = (jnp.arange(slots, dtype=jnp.int32) < tile_count).astype(jnp.float32)
    onehot = (tile_cols[:, None] == jnp.arange(panel_count, dtype=jnp.int32)[None, :]).astype(
        jnp.float32
    )
    onehot = onehot * live[:, None]
    counts = jnp.einsum("kp,kit->ipt", onehot, tile_mask.astype(jnp.float32))
    counts = counts.reshape(block_rows, panel_count * tile_width)
    return (counts * lax.rsqrt(degree.astype(jnp.float32))[:, None]).astype(jnp.bfloat16)


def body(features, weight, cotangent, tile_mask, tile_cols, tile_count, degree):
    f32, bf16 = jnp.float32, jnp.bfloat16
    node_rows, width = features.shape[2], features.shape[3]
    rows = lax.axis_size(ROW)
    depth = lax.axis_size("z")
    cube = lax.axis_size(CUBE)
    part = width // MEMBERS
    col_nodes = rows * node_rows
    block_rows = tile_mask.shape[3]

    own = features[0, 0].reshape(node_rows, MEMBERS, part).transpose(1, 0, 2)
    send = jnp.broadcast_to(own[None], (rows // MEMBERS, MEMBERS, node_rows, part))
    panels = lax.all_to_all(send.reshape(rows, node_rows, part), ROW, 0, 0)
    panels = panels.reshape(col_nodes, part)

    dense = dense_of(
        tile_mask[0, 0], tile_cols[0, 0], tile_count[0, 0], degree[0], col_nodes // tile_mask.shape[4]
    )
    across = lax.ppermute(dense, "xl", SWAP)
    blocks = [dense, lax.ppermute(dense, "core", SWAP), across, lax.ppermute(across, "core", SWAP)]

    partial = [jnp.dot(b, panels, preferred_element_type=f32).astype(bf16) for b in blocks]
    partial = jnp.stack(exclusive(partial)).reshape(MEMBERS * depth, node_rows, part)
    sums = lax.all_to_all(partial, TEAM, 0, 0).reshape(MEMBERS, depth, node_rows, part)
    sums = jnp.sum(sums.astype(f32), axis=1)
    own_inputs = jnp.concatenate([sums[m] for m in range(MEMBERS)], axis=1).astype(bf16)

    own_pre = jnp.dot(own_inputs, weight, preferred_element_type=f32)
    activated = jax.nn.silu(own_pre).astype(bf16)
    own_slope = (cotangent[0, 0].astype(f32) * slope_of(own_pre)).astype(bf16)
    own_proj = lax.dot_general(
        own_slope, weight, (((1,), (1,)), ((), ())), preferred_element_type=f32
    ).astype(bf16)

    lanes = 128
    share = width // depth
    per_lane = lanes // share
    quarters = jnp.stack(
        [
            jnp.concatenate(
                [own_proj[:, m * part : (m + 1) * part], own_slope[:, m * part : (m + 1) * part]], axis=1
            )
            for m in range(MEMBERS)
        ]
    )
    slices = jnp.stack(
        [own_inputs[:, (d // per_lane) * lanes : (d // per_lane + 1) * lanes] for d in range(depth)]
    )
    both = jnp.concatenate(
        [
            jnp.broadcast_to(quarters[:, None], (MEMBERS, depth, node_rows, 2 * part)),
            jnp.broadcast_to(slices[None], (MEMBERS, depth, node_rows, lanes)),
        ],
        axis=3,
    ).reshape(MEMBERS * depth, node_rows, 2 * part + lanes)
    both = lax.all_to_all(both, TEAM, 0, 0).reshape(MEMBERS * block_rows, 2 * part + lanes)
    proj = exclusive(both[:, :part].reshape(MEMBERS, block_rows, part))
    contract_rows = (((0,), (0,)), ((), ()))
    grad = sum(
        lax.dot_general(b, p, contract_rows, preferred_element_type=f32)
        for b, p in zip(blocks, proj, strict=True)
    )
    grad = grad.astype(bf16).reshape(rows, node_rows, part)
    term = lax.dot_general(
        both[:, 2 * part :], both[:, part : 2 * part], contract_rows, preferred_element_type=f32
    )
    term = term.reshape(per_lane, share, part)
    term = lax.dynamic_index_in_dim(term, lax.axis_index("z") % per_lane, 0, keepdims=False)
    extra = share // cube
    term = term.astype(bf16).reshape(1, 2, 1, MEMBERS, extra, part)
    term = jnp.broadcast_to(term, (rows // (8 * MEMBERS), 2, 4, MEMBERS, extra, part))
    term = term.reshape(rows, extra, part)
    out = lax.all_to_all(jnp.concatenate([grad, term], axis=1), ROW, 0, 0)
    out = out.reshape(rows // MEMBERS, MEMBERS, node_rows + extra, part)
    total = jnp.sum(out[:, :, :node_rows].astype(f32), axis=0)
    feature_grad = jnp.concatenate([total[m] for m in range(MEMBERS)], axis=1).astype(bf16)
    weight_rows = jnp.sum(out[:, :, node_rows:].astype(f32), axis=0)
    weight_rows = jnp.concatenate([weight_rows[m] for m in range(MEMBERS)], axis=1)
    weight_grad = lax.all_to_all(jnp.broadcast_to(weight_rows[None], (cube, extra, width)), CUBE, 0, 0)
    return (
        activated.reshape(1, 1, node_rows, width),
        feature_grad.reshape(1, 1, node_rows, width),
        weight_grad.reshape(share, width),
    )


def solution(mesh):
    fine = Mesh(mesh.devices.reshape(4, 2, 4, 2, 2, 8), ROW + ("z",))
    in_specs = (
        P("z", ROW, None, None),
        P(),
        P(ROW, "z", None, None),
        P(ROW, "z", None, None, None),
        P(ROW, "z", None),
        P(ROW, "z"),
        P(ROW, None),
    )
    out_specs = (P(ROW, "z", None, None), P("z", ROW, None, None), P("z", None))
    return jax.shard_map(body, mesh=fine, in_specs=in_specs, out_specs=out_specs, check_vma=False)
```

```python
import jax
import jax.numpy as jnp
from jax import lax
from jax.experimental import pallas as pl
from jax.experimental.pallas import tpu as pltpu
from jax.sharding import Mesh, PartitionSpec as P

ROW = ("yh", "yl", "xh", "xl", "core")
CUBE = ("yl", "xl", "core")
TEAM = ("xl", "core", "z")
SWAP = [(0, 1), (1, 0)]
MEMBERS = 4


def exclusive(blocks):
    core = lax.axis_index("core") == 1
    half = lax.axis_index("xl") == 1
    a, b, c, d = (blocks[i] for i in range(MEMBERS))
    a, b, c, d = (
        jnp.where(core, b, a),
        jnp.where(core, a, b),
        jnp.where(core, d, c),
        jnp.where(core, c, d),
    )
    return [
        jnp.where(half, c, a),
        jnp.where(half, d, b),
        jnp.where(half, a, c),
        jnp.where(half, b, d),
    ]


def local(kernel, out, ins, flops, moved, operands, scratch=()):
    return pl.pallas_call(
        kernel,
        out_shape=out,
        in_specs=[pl.BlockSpec(memory_space=space) for space in ins],
        scratch_shapes=scratch,
        cost_estimate=pl.CostEstimate(flops=flops, bytes_accessed=moved, transcendentals=0),
        compiler_params=pltpu.CompilerParams(vmem_limit_bytes=32 * 2**20),
    )(*operands)


def spread_kernel(own_ref, out_ref):
    groups, members, node_rows, part = out_ref.shape
    for m in range(members):
        quarter = own_ref[:, m * part : (m + 1) * part]
        out_ref[:, m] = jnp.broadcast_to(quarter[None], (groups, node_rows, part))


def compact_kernel(count_ref, cols_ref, scale_ref, mask_ref, out_ref):
    slots, block_rows, tile_width = mask_ref.shape
    scale = jnp.broadcast_to(scale_ref[...], (block_rows, block_rows)).T
    count = count_ref[0]
    for s in range(slots):
        kept = scale * (s < count).astype(jnp.float32)
        tile = mask_ref[s].astype(jnp.float32) * kept
        out_ref[s * block_rows : (s + 1) * block_rows, :] = tile.astype(jnp.bfloat16)
    tail = out_ref.shape[0] - slots * block_rows
    row = lax.broadcasted_iota(jnp.int32, (tail, tile_width), 0)
    place = jnp.zeros((tail, tile_width), jnp.int32)
    for s in range(slots):
        place = jnp.where(row == s, cols_ref[s], place)
    out_ref[slots * block_rows :, :] = place.astype(jnp.float32).astype(jnp.bfloat16)


def place_kernel(tiles_ref, out_ref):
    block_rows = out_ref.shape[0]
    tile_width = tiles_ref.shape[1]
    slots = tiles_ref.shape[0] // block_rows
    out_ref[...] = jnp.zeros_like(out_ref)
    place = tiles_ref[slots * block_rows :, :].astype(jnp.float32)
    for s in range(slots):
        col = jnp.max(place[s : s + 1, :]).astype(jnp.int32)
        start = pl.multiple_of(col * tile_width, tile_width)
        out_ref[:, pl.ds(start, tile_width)] = tiles_ref[s * block_rows : (s + 1) * block_rows, :]


def node_kernel(sums_ref, weight_ref, cotangent_ref, active_ref, out_ref):
    f32, bf16 = jnp.float32, jnp.bfloat16
    members, depth, node_rows, part = sums_ref.shape
    width = members * part
    lanes = out_ref.shape[2] - 2 * part
    sums = [jnp.sum(sums_ref[m].astype(f32), axis=0).astype(bf16) for m in range(members)]
    own_inputs = jnp.concatenate(sums, axis=1)
    pre = jnp.dot(own_inputs, weight_ref[...], preferred_element_type=f32)
    sigma = 1.0 / (1.0 + jnp.exp(-pre))
    active_ref[...] = (pre * sigma).astype(bf16)
    slope = cotangent_ref[...].astype(f32) * (sigma * (1.0 + pre * (1.0 - sigma)))
    slope = slope.astype(bf16)
    proj = lax.dot_general(
        slope, weight_ref[...], (((1,), (1,)), ((), ())), preferred_element_type=f32
    ).astype(bf16)
    for m in range(members):
        for d in range(depth):
            first = d * (width // depth) // lanes * lanes
            at = m * depth + d
            out_ref[at, :, :part] = proj[:, m * part : (m + 1) * part]
            out_ref[at, :, part : 2 * part] = slope[:, m * part : (m + 1) * part]
            out_ref[at, :, 2 * part :] = own_inputs[:, first : first + lanes]


def body(features, weight, cotangent, tile_mask, tile_cols, tile_count, degree):
    f32, bf16 = jnp.float32, jnp.bfloat16
    node_rows, width = features.shape[2], features.shape[3]
    rows = lax.axis_size(ROW)
    depth = lax.axis_size("z")
    cube = lax.axis_size(CUBE)
    part = width // MEMBERS
    col_nodes = rows * node_rows
    block_rows = tile_mask.shape[3]

    vmem, smem = pltpu.VMEM, pltpu.SMEM
    send = local(
        spread_kernel,
        jax.ShapeDtypeStruct((rows // MEMBERS, MEMBERS, node_rows, part), bf16),
        [vmem],
        0,
        2 * col_nodes * part,
        [features[0, 0]],
    )
    panels = lax.all_to_all(send.reshape(rows, node_rows, part), ROW, 0, 0)
    panels = panels.reshape(col_nodes, part)

    slots, tile_width = tile_mask.shape[2], tile_mask.shape[4]
    tiles = local(
        compact_kernel,
        jax.ShapeDtypeStruct((slots * block_rows + 16, tile_width), bf16),
        [smem, smem, vmem, vmem],
        2 * slots * block_rows * tile_width,
        6 * slots * block_rows * tile_width,
        [tile_count[0], tile_cols[0, 0], lax.rsqrt(degree.astype(f32)), tile_mask[0, 0]],
    )
    across = lax.ppermute(tiles, "xl", SWAP)
    blocks = [
        local(
            place_kernel,
            jax.ShapeDtypeStruct((block_rows, col_nodes), bf16),
            [vmem],
            0,
            2 * (slots + 2 * col_nodes // tile_width) * block_rows * tile_width,
            [block],
        )
        for block in (tiles, lax.ppermute(tiles, "core", SWAP), across, lax.ppermute(across, "core", SWAP))
    ]

    partial = [jnp.dot(b, panels, preferred_element_type=f32).astype(bf16) for b in blocks]
    partial = jnp.stack(exclusive(partial)).reshape(MEMBERS * depth, node_rows, part)
    sums = lax.all_to_all(partial, TEAM, 0, 0).reshape(MEMBERS, depth, node_rows, part)
    lanes = 128
    share = width // depth
    per_lane = lanes // share
    activated, both = local(
        node_kernel,
        (
            jax.ShapeDtypeStruct((node_rows, width), bf16),
            jax.ShapeDtypeStruct((MEMBERS * depth, node_rows, 2 * part + lanes), bf16),
        ),
        [vmem, vmem, vmem],
        4 * node_rows * width * width,
        2 * width * width + 8 * col_nodes * part,
        [sums, weight, cotangent[0, 0]],
    )
    both = lax.all_to_all(both, TEAM, 0, 0).reshape(MEMBERS * block_rows, 2 * part + lanes)
    proj = exclusive(both[:, :part].reshape(MEMBERS, block_rows, part))
    contract_rows = (((0,), (0,)), ((), ()))
    grad = sum(
        lax.dot_general(b, p, contract_rows, preferred_element_type=f32)
        for b, p in zip(blocks, proj, strict=True)
    )
    grad = grad.astype(bf16).reshape(rows, node_rows, part)
    term = lax.dot_general(
        both[:, 2 * part :], both[:, part : 2 * part], contract_rows, preferred_element_type=f32
    )
    term = term.reshape(per_lane, share, part)
    term = lax.dynamic_index_in_dim(term, lax.axis_index("z") % per_lane, 0, keepdims=False)
    extra = share // cube
    term = term.astype(bf16).reshape(1, 2, 1, MEMBERS, extra, part)
    term = jnp.broadcast_to(term, (rows // (8 * MEMBERS), 2, 4, MEMBERS, extra, part))
    term = term.reshape(rows, extra, part)
    out = lax.all_to_all(jnp.concatenate([grad, term], axis=1), ROW, 0, 0)
    out = out.reshape(rows // MEMBERS, MEMBERS, node_rows + extra, part)
    total = jnp.sum(out[:, :, :node_rows].astype(f32), axis=0)
    feature_grad = jnp.concatenate([total[m] for m in range(MEMBERS)], axis=1).astype(bf16)
    weight_rows = jnp.sum(out[:, :, node_rows:].astype(f32), axis=0)
    weight_rows = jnp.concatenate([weight_rows[m] for m in range(MEMBERS)], axis=1)
    weight_grad = lax.all_to_all(jnp.broadcast_to(weight_rows[None], (cube, extra, width)), CUBE, 0, 0)
    return (
        activated.reshape(1, 1, node_rows, width),
        feature_grad.reshape(1, 1, node_rows, width),
        weight_grad.reshape(share, width),
    )


def solution(mesh):
    fine = Mesh(mesh.devices.reshape(4, 2, 4, 2, 2, 8), ROW + ("z",))
    in_specs = (
        P("z", ROW, None, None),
        P(),
        P(ROW, "z", None, None),
        P(ROW, "z", None, None, None),
        P(ROW, "z", None),
        P(ROW, "z"),
        P(ROW, None),
    )
    out_specs = (P(ROW, "z", None, None), P("z", ROW, None, None), P("z", None))
    return jax.shard_map(body, mesh=fine, in_specs=in_specs, out_specs=out_specs, check_vma=False)
```

```python
import jax
import jax.numpy as jnp
from jax import lax
from jax.experimental import pallas as pl
from jax.experimental.pallas import tpu as pltpu
from jax.sharding import Mesh, PartitionSpec as P

ROW = ("yh", "yl", "xh", "xl", "core")
CUBE = ("yl", "xl", "core")
TEAM = ("xl", "core", "z")
SWAP = [(0, 1), (1, 0)]
MEMBERS = 4


def exclusive(blocks):
    core = lax.axis_index("core") == 1
    half = lax.axis_index("xl") == 1
    a, b, c, d = (blocks[i] for i in range(MEMBERS))
    a, b, c, d = (
        jnp.where(core, b, a),
        jnp.where(core, a, b),
        jnp.where(core, d, c),
        jnp.where(core, c, d),
    )
    return [
        jnp.where(half, c, a),
        jnp.where(half, d, b),
        jnp.where(half, a, c),
        jnp.where(half, b, d),
    ]


def local(kernel, out, ins, flops, moved, operands, scratch=()):
    return pl.pallas_call(
        kernel,
        out_shape=out,
        in_specs=[pl.BlockSpec(memory_space=space) for space in ins],
        scratch_shapes=scratch,
        cost_estimate=pl.CostEstimate(flops=flops, bytes_accessed=moved, transcendentals=0),
        compiler_params=pltpu.CompilerParams(vmem_limit_bytes=32 * 2**20),
    )(*operands)


def spread_kernel(own_ref, out_ref):
    groups, members, node_rows, part = out_ref.shape
    for m in range(members):
        quarter = own_ref[:, m * part : (m + 1) * part]
        out_ref[:, m] = jnp.broadcast_to(quarter[None], (groups, node_rows, part))


def compact_kernel(count_ref, cols_ref, scale_ref, mask_ref, out_ref):
    slots, block_rows, tile_width = mask_ref.shape
    scale = jnp.broadcast_to(scale_ref[...], (block_rows, block_rows)).T
    count = count_ref[0]
    for s in range(slots):
        kept = scale * (s < count).astype(jnp.float32)
        tile = mask_ref[s].astype(jnp.float32) * kept
        out_ref[s * block_rows : (s + 1) * block_rows, :] = tile.astype(jnp.bfloat16)
    tail = out_ref.shape[0] - slots * block_rows
    row = lax.broadcasted_iota(jnp.int32, (tail, tile_width), 0)
    place = jnp.zeros((tail, tile_width), jnp.int32)
    for s in range(slots):
        place = jnp.where(row == s, cols_ref[s], place)
    out_ref[slots * block_rows :, :] = place.astype(jnp.float32).astype(jnp.bfloat16)


def place_kernel(tiles_ref, out_ref):
    block_rows = out_ref.shape[0]
    tile_width = tiles_ref.shape[1]
    slots = tiles_ref.shape[0] // block_rows
    out_ref[...] = jnp.zeros_like(out_ref)
    place = tiles_ref[slots * block_rows :, :].astype(jnp.float32)
    for s in range(slots):
        col = jnp.max(place[s : s + 1, :]).astype(jnp.int32)
        start = pl.multiple_of(col * tile_width, tile_width)
        out_ref[:, pl.ds(start, tile_width)] = tiles_ref[s * block_rows : (s + 1) * block_rows, :]


def node_kernel(sums_ref, weight_ref, cotangent_ref, active_ref, out_ref):
    f32, bf16 = jnp.float32, jnp.bfloat16
    members, depth, node_rows, part = sums_ref.shape
    width = members * part
    lanes = out_ref.shape[2]
    share = width // depth
    few = node_rows // 2
    left = lax.broadcasted_iota(jnp.int32, (few, lanes), 1) < share
    sums = [jnp.sum(sums_ref[m].astype(f32), axis=0).astype(bf16) for m in range(members)]
    own_inputs = jnp.concatenate(sums, axis=1)
    pre = jnp.dot(own_inputs, weight_ref[...], preferred_element_type=f32)
    sigma = 1.0 / (1.0 + jnp.exp(-pre))
    active_ref[...] = (pre * sigma).astype(bf16)
    slope = cotangent_ref[...].astype(f32) * (sigma * (1.0 + pre * (1.0 - sigma)))
    slope = slope.astype(bf16)
    proj = lax.dot_general(
        slope, weight_ref[...], (((1,), (1,)), ((), ())), preferred_element_type=f32
    ).astype(bf16)
    packed = []
    for d in range(depth):
        first = d * share // lanes * lanes
        both = own_inputs[:, first : first + lanes].astype(f32)
        early, late = both[:few], both[few:]
        if d * share == first:
            pair = jnp.where(left, early, pltpu.roll(late, share, 1))
        else:
            pair = jnp.where(left, pltpu.roll(early, share, 1), late)
        packed.append(pair.astype(bf16))
    for m in range(members):
        for d in range(depth):
            at = m * depth + d
            out_ref[at, :node_rows] = proj[:, m * part : (m + 1) * part]
            out_ref[at, node_rows : 2 * node_rows] = slope[:, m * part : (m + 1) * part]
            out_ref[at, 2 * node_rows :] = packed[d]


def body(features, weight, cotangent, tile_mask, tile_cols, tile_count, degree):
    f32, bf16 = jnp.float32, jnp.bfloat16
    node_rows, width = features.shape[2], features.shape[3]
    rows = lax.axis_size(ROW)
    depth = lax.axis_size("z")
    cube = lax.axis_size(CUBE)
    part = width // MEMBERS
    col_nodes = rows * node_rows
    block_rows = tile_mask.shape[3]

    vmem, smem = pltpu.VMEM, pltpu.SMEM
    send = local(
        spread_kernel,
        jax.ShapeDtypeStruct((rows // MEMBERS, MEMBERS, node_rows, part), bf16),
        [vmem],
        0,
        2 * col_nodes * part,
        [features[0, 0]],
    )
    panels = lax.all_to_all(send.reshape(rows, node_rows, part), ROW, 0, 0)
    panels = panels.reshape(col_nodes, part)

    slots, tile_width = tile_mask.shape[2], tile_mask.shape[4]
    tiles = local(
        compact_kernel,
        jax.ShapeDtypeStruct((slots * block_rows + 16, tile_width), bf16),
        [smem, smem, vmem, vmem],
        2 * slots * block_rows * tile_width,
        6 * slots * block_rows * tile_width,
        [tile_count[0], tile_cols[0, 0], lax.rsqrt(degree.astype(f32)), tile_mask[0, 0]],
    )
    across = lax.ppermute(tiles, "xl", SWAP)
    blocks = [
        local(
            place_kernel,
            jax.ShapeDtypeStruct((block_rows, col_nodes), bf16),
            [vmem],
            0,
            2 * (slots + 2 * col_nodes // tile_width) * block_rows * tile_width,
            [block],
        )
        for block in (tiles, lax.ppermute(tiles, "core", SWAP), across, lax.ppermute(across, "core", SWAP))
    ]

    partial = [jnp.dot(b, panels, preferred_element_type=f32).astype(bf16) for b in blocks]
    partial = jnp.stack(exclusive(partial)).reshape(MEMBERS * depth, node_rows, part)
    sums = lax.all_to_all(partial, TEAM, 0, 0).reshape(MEMBERS, depth, node_rows, part)
    share = width // depth
    few = node_rows // 2
    tall = 2 * node_rows + few
    activated, both = local(
        node_kernel,
        (
            jax.ShapeDtypeStruct((node_rows, width), bf16),
            jax.ShapeDtypeStruct((MEMBERS * depth, tall, part), bf16),
        ),
        [vmem, vmem, vmem],
        4 * node_rows * width * width,
        2 * width * width + 8 * col_nodes * part,
        [sums, weight, cotangent[0, 0]],
    )
    both = lax.all_to_all(both, TEAM, 0, 0)
    proj = exclusive(both[:, :node_rows].reshape(MEMBERS, block_rows, part))
    contract_rows = (((0,), (0,)), ((), ()))
    grad = sum(
        lax.dot_general(b, p, contract_rows, preferred_element_type=f32)
        for b, p in zip(blocks, proj, strict=True)
    )
    grad = grad.astype(bf16).reshape(rows, node_rows, part)
    slope = both[:, node_rows : 2 * node_rows].reshape(-1, 2, few, part)
    slope = jnp.concatenate([slope[:, 0], slope[:, 1]], axis=2).reshape(-1, 2 * part)
    packed = both[:, 2 * node_rows :].reshape(-1, part)
    term = lax.dot_general(packed, slope, contract_rows, preferred_element_type=f32)
    term = term[:share, :part] + term[share:, part:]
    extra = share // cube
    term = term.astype(bf16).reshape(1, 2, 1, MEMBERS, extra, part)
    term = jnp.broadcast_to(term, (rows // (8 * MEMBERS), 2, 4, MEMBERS, extra, part))
    term = term.reshape(rows, extra, part)
    out = lax.all_to_all(jnp.concatenate([grad, term], axis=1), ROW, 0, 0)
    out = out.reshape(rows // MEMBERS, MEMBERS, node_rows + extra, part)
    total = jnp.sum(out[:, :, :node_rows].astype(f32), axis=0)
    feature_grad = jnp.concatenate([total[m] for m in range(MEMBERS)], axis=1).astype(bf16)
    weight_rows = jnp.sum(out[:, :, node_rows:].astype(f32), axis=0)
    weight_rows = jnp.concatenate([weight_rows[m] for m in range(MEMBERS)], axis=1)
    weight_grad = lax.all_to_all(jnp.broadcast_to(weight_rows[None], (cube, extra, width)), CUBE, 0, 0)
    return (
        activated.reshape(1, 1, node_rows, width),
        feature_grad.reshape(1, 1, node_rows, width),
        weight_grad.reshape(share, width),
    )


def solution(mesh):
    fine = Mesh(mesh.devices.reshape(4, 2, 4, 2, 2, 8), ROW + ("z",))
    in_specs = (
        P("z", ROW, None, None),
        P(),
        P(ROW, "z", None, None),
        P(ROW, "z", None, None, None),
        P(ROW, "z", None),
        P(ROW, "z"),
        P(ROW, None),
    )
    out_specs = (P(ROW, "z", None, None), P("z", ROW, None, None), P("z", None))
    return jax.shard_map(body, mesh=fine, in_specs=in_specs, out_specs=out_specs, check_vma=False)
```

```python
import jax
import jax.numpy as jnp
from jax import lax
from jax.experimental import pallas as pl
from jax.experimental.pallas import tpu as pltpu
from jax.sharding import Mesh, PartitionSpec as P

ROW = ("yh", "yl", "xh", "xl", "core")
CUBE = ("yl", "xl", "core")
TEAM = ("xl", "core", "z")
SWAP = [(0, 1), (1, 0)]
MEMBERS = 4


def exclusive(blocks):
    core = lax.axis_index("core") == 1
    half = lax.axis_index("xl") == 1
    a, b, c, d = (blocks[i] for i in range(MEMBERS))
    a, b, c, d = (
        jnp.where(core, b, a),
        jnp.where(core, a, b),
        jnp.where(core, d, c),
        jnp.where(core, c, d),
    )
    return [
        jnp.where(half, c, a),
        jnp.where(half, d, b),
        jnp.where(half, a, c),
        jnp.where(half, b, d),
    ]


def local(kernel, out, ins, flops, moved, operands, scratch=()):
    return pl.pallas_call(
        kernel,
        out_shape=out,
        in_specs=[pl.BlockSpec(memory_space=space) for space in ins],
        scratch_shapes=scratch,
        cost_estimate=pl.CostEstimate(flops=flops, bytes_accessed=moved, transcendentals=0),
        compiler_params=pltpu.CompilerParams(vmem_limit_bytes=32 * 2**20),
    )(*operands)


def spread_kernel(own_ref, out_ref):
    groups, members, node_rows, part = out_ref.shape
    for m in range(members):
        quarter = own_ref[:, m * part : (m + 1) * part]
        out_ref[:, m] = jnp.broadcast_to(quarter[None], (groups, node_rows, part))


def compact_kernel(count_ref, cols_ref, scale_ref, mask_ref, out_ref):
    slots, block_rows, tile_width = mask_ref.shape
    scale = jnp.broadcast_to(scale_ref[...], (block_rows, block_rows)).T
    count = count_ref[0]
    for s in range(slots):
        kept = scale * (s < count).astype(jnp.float32)
        tile = mask_ref[s].astype(jnp.float32) * kept
        out_ref[s * block_rows : (s + 1) * block_rows, :] = tile.astype(jnp.bfloat16)
    tail = out_ref.shape[0] - slots * block_rows
    row = lax.broadcasted_iota(jnp.int32, (tail, tile_width), 0)
    place = jnp.zeros((tail, tile_width), jnp.int32)
    for s in range(slots):
        place = jnp.where(row == s, cols_ref[s], place)
    out_ref[slots * block_rows :, :] = place.astype(jnp.float32).astype(jnp.bfloat16)


def place_kernel(tiles_ref, out_ref):
    block_rows = out_ref.shape[0]
    tile_width = tiles_ref.shape[1]
    slots = tiles_ref.shape[0] // block_rows
    out_ref[...] = jnp.zeros_like(out_ref)
    place = tiles_ref[slots * block_rows :, :].astype(jnp.float32)
    for s in range(slots):
        col = jnp.max(place[s : s + 1, :]).astype(jnp.int32)
        start = pl.multiple_of(col * tile_width, tile_width)
        out_ref[:, pl.ds(start, tile_width)] = tiles_ref[s * block_rows : (s + 1) * block_rows, :]


def forward_kernel(*refs):
    *block_refs, panels_ref, out_ref = refs
    me = lax.axis_index("xl") * 2 + lax.axis_index("core")
    for other, block_ref in enumerate(block_refs):
        product = jnp.dot(block_ref[...], panels_ref[...], preferred_element_type=jnp.float32)
        out_ref[lax.bitwise_xor(me, other)] = product.astype(jnp.bfloat16)


def node_kernel(sums_ref, weight_ref, cotangent_ref, active_ref, out_ref):
    f32, bf16 = jnp.float32, jnp.bfloat16
    members, depth, node_rows, part = sums_ref.shape
    width = members * part
    lanes = out_ref.shape[2]
    share = width // depth
    few = node_rows // 2
    left = lax.broadcasted_iota(jnp.int32, (few, lanes), 1) < share
    sums = [jnp.sum(sums_ref[m].astype(f32), axis=0).astype(bf16) for m in range(members)]
    own_inputs = jnp.concatenate(sums, axis=1)
    pre = jnp.dot(own_inputs, weight_ref[...], preferred_element_type=f32)
    sigma = 1.0 / (1.0 + jnp.exp(-pre))
    active_ref[...] = (pre * sigma).astype(bf16)
    slope = cotangent_ref[...].astype(f32) * (sigma * (1.0 + pre * (1.0 - sigma)))
    slope = slope.astype(bf16)
    proj = lax.dot_general(
        slope, weight_ref[...], (((1,), (1,)), ((), ())), preferred_element_type=f32
    ).astype(bf16)
    packed = []
    for d in range(depth):
        first = d * share // lanes * lanes
        both = own_inputs[:, first : first + lanes].astype(f32)
        early, late = both[:few], both[few:]
        if d * share == first:
            pair = jnp.where(left, early, pltpu.roll(late, share, 1))
        else:
            pair = jnp.where(left, pltpu.roll(early, share, 1), late)
        packed.append(pair.astype(bf16))
    for m in range(members):
        for d in range(depth):
            at = m * depth + d
            out_ref[at, :node_rows] = proj[:, m * part : (m + 1) * part]
            out_ref[at, node_rows : 2 * node_rows] = slope[:, m * part : (m + 1) * part]
            out_ref[at, 2 * node_rows :] = packed[d]


def body(features, weight, cotangent, tile_mask, tile_cols, tile_count, degree):
    f32, bf16 = jnp.float32, jnp.bfloat16
    node_rows, width = features.shape[2], features.shape[3]
    rows = lax.axis_size(ROW)
    depth = lax.axis_size("z")
    cube = lax.axis_size(CUBE)
    part = width // MEMBERS
    col_nodes = rows * node_rows
    block_rows = tile_mask.shape[3]

    vmem, smem = pltpu.VMEM, pltpu.SMEM
    send = local(
        spread_kernel,
        jax.ShapeDtypeStruct((rows // MEMBERS, MEMBERS, node_rows, part), bf16),
        [vmem],
        0,
        2 * col_nodes * part,
        [features[0, 0]],
    )
    panels = lax.all_to_all(send.reshape(rows, node_rows, part), ROW, 0, 0)
    panels = panels.reshape(col_nodes, part)

    slots, tile_width = tile_mask.shape[2], tile_mask.shape[4]
    tiles = local(
        compact_kernel,
        jax.ShapeDtypeStruct((slots * block_rows + 16, tile_width), bf16),
        [smem, smem, vmem, vmem],
        2 * slots * block_rows * tile_width,
        6 * slots * block_rows * tile_width,
        [tile_count[0], tile_cols[0, 0], lax.rsqrt(degree.astype(f32)), tile_mask[0, 0]],
    )
    across = lax.ppermute(tiles, "xl", SWAP)
    blocks = [
        local(
            place_kernel,
            jax.ShapeDtypeStruct((block_rows, col_nodes), bf16),
            [vmem],
            0,
            2 * (slots + 2 * col_nodes // tile_width) * block_rows * tile_width,
            [block],
        )
        for block in (tiles, lax.ppermute(tiles, "core", SWAP), across, lax.ppermute(across, "core", SWAP))
    ]

    partial = local(
        forward_kernel,
        jax.ShapeDtypeStruct((MEMBERS, block_rows, part), bf16),
        [vmem] * (MEMBERS + 1),
        2 * MEMBERS * block_rows * col_nodes * part,
        2 * (MEMBERS * block_rows + part) * col_nodes,
        [*blocks, panels],
    ).reshape(MEMBERS * depth, node_rows, part)
    sums = lax.all_to_all(partial, TEAM, 0, 0).reshape(MEMBERS, depth, node_rows, part)
    share = width // depth
    few = node_rows // 2
    tall = 2 * node_rows + few
    activated, both = local(
        node_kernel,
        (
            jax.ShapeDtypeStruct((node_rows, width), bf16),
            jax.ShapeDtypeStruct((MEMBERS * depth, tall, part), bf16),
        ),
        [vmem, vmem, vmem],
        4 * node_rows * width * width,
        2 * width * width + 8 * col_nodes * part,
        [sums, weight, cotangent[0, 0]],
    )
    both = lax.all_to_all(both, TEAM, 0, 0)
    proj = exclusive(both[:, :node_rows].reshape(MEMBERS, block_rows, part))
    contract_rows = (((0,), (0,)), ((), ()))
    grad = sum(
        lax.dot_general(b, p, contract_rows, preferred_element_type=f32)
        for b, p in zip(blocks, proj, strict=True)
    )
    grad = grad.astype(bf16).reshape(rows, node_rows, part)
    slope = both[:, node_rows : 2 * node_rows].reshape(-1, 2, few, part)
    slope = jnp.concatenate([slope[:, 0], slope[:, 1]], axis=2).reshape(-1, 2 * part)
    packed = both[:, 2 * node_rows :].reshape(-1, part)
    term = lax.dot_general(packed, slope, contract_rows, preferred_element_type=f32)
    term = term[:share, :part] + term[share:, part:]
    extra = share // cube
    term = term.astype(bf16).reshape(1, 2, 1, MEMBERS, extra, part)
    term = jnp.broadcast_to(term, (rows // (8 * MEMBERS), 2, 4, MEMBERS, extra, part))
    term = term.reshape(rows, extra, part)
    out = lax.all_to_all(jnp.concatenate([grad, term], axis=1), ROW, 0, 0)
    out = out.reshape(rows // MEMBERS, MEMBERS, node_rows + extra, part)
    total = jnp.sum(out[:, :, :node_rows].astype(f32), axis=0)
    feature_grad = jnp.concatenate([total[m] for m in range(MEMBERS)], axis=1).astype(bf16)
    weight_rows = jnp.sum(out[:, :, node_rows:].astype(f32), axis=0)
    weight_rows = jnp.concatenate([weight_rows[m] for m in range(MEMBERS)], axis=1)
    weight_grad = lax.all_to_all(jnp.broadcast_to(weight_rows[None], (cube, extra, width)), CUBE, 0, 0)
    return (
        activated.reshape(1, 1, node_rows, width),
        feature_grad.reshape(1, 1, node_rows, width),
        weight_grad.reshape(share, width),
    )


def solution(mesh):
    fine = Mesh(mesh.devices.reshape(4, 2, 4, 2, 2, 8), ROW + ("z",))
    in_specs = (
        P("z", ROW, None, None),
        P(),
        P(ROW, "z", None, None),
        P(ROW, "z", None, None, None),
        P(ROW, "z", None),
        P(ROW, "z"),
        P(ROW, None),
    )
    out_specs = (P(ROW, "z", None, None), P("z", ROW, None, None), P("z", None))
    return jax.shard_map(body, mesh=fine, in_specs=in_specs, out_specs=out_specs, check_vma=False)
```

```python
import jax
import jax.numpy as jnp
from jax import lax
from jax.experimental import pallas as pl
from jax.experimental.pallas import tpu as pltpu
from jax.sharding import Mesh, PartitionSpec as P

ROW = ("yh", "yl", "xh", "xl", "core")
CUBE = ("yl", "xl", "core")
TEAM = ("xl", "core", "z")
SWAP = [(0, 1), (1, 0)]
MEMBERS = 4


def exclusive(blocks, core, half):
    a, b, c, d = (blocks[i] for i in range(MEMBERS))
    a, b, c, d = (
        jnp.where(core, b, a),
        jnp.where(core, a, b),
        jnp.where(core, d, c),
        jnp.where(core, c, d),
    )
    return [
        jnp.where(half, c, a),
        jnp.where(half, d, b),
        jnp.where(half, a, c),
        jnp.where(half, b, d),
    ]


def local(kernel, out, ins, flops, moved, operands, scratch=()):
    return pl.pallas_call(
        kernel,
        out_shape=out,
        in_specs=[pl.BlockSpec(memory_space=space) for space in ins],
        scratch_shapes=scratch,
        cost_estimate=pl.CostEstimate(flops=flops, bytes_accessed=moved, transcendentals=0),
        compiler_params=pltpu.CompilerParams(vmem_limit_bytes=32 * 2**20),
    )(*operands)


def spread_kernel(own_ref, out_ref):
    groups, members, node_rows, part = out_ref.shape
    for m in range(members):
        quarter = own_ref[:, m * part : (m + 1) * part]
        out_ref[:, m] = jnp.broadcast_to(quarter[None], (groups, node_rows, part))


def compact_kernel(count_ref, cols_ref, scale_ref, mask_ref, out_ref):
    slots, block_rows, tile_width = mask_ref.shape
    scale = jnp.broadcast_to(scale_ref[...], (block_rows, block_rows)).T
    count = count_ref[0]
    for s in range(slots):
        kept = scale * (s < count).astype(jnp.float32)
        tile = mask_ref[s].astype(jnp.float32) * kept
        out_ref[s * block_rows : (s + 1) * block_rows, :] = tile.astype(jnp.bfloat16)
    tail = out_ref.shape[0] - slots * block_rows
    row = lax.broadcasted_iota(jnp.int32, (tail, tile_width), 0)
    place = jnp.zeros((tail, tile_width), jnp.int32)
    for s in range(slots):
        place = jnp.where(row == s, cols_ref[s], place)
    out_ref[slots * block_rows :, :] = place.astype(jnp.float32).astype(jnp.bfloat16)


def place_kernel(tiles_ref, out_ref):
    block_rows = out_ref.shape[0]
    tile_width = tiles_ref.shape[1]
    slots = tiles_ref.shape[0] // block_rows
    out_ref[...] = jnp.zeros_like(out_ref)
    place = tiles_ref[slots * block_rows :, :].astype(jnp.float32)
    for s in range(slots):
        col = jnp.max(place[s : s + 1, :]).astype(jnp.int32)
        start = pl.multiple_of(col * tile_width, tile_width)
        out_ref[:, pl.ds(start, tile_width)] = tiles_ref[s * block_rows : (s + 1) * block_rows, :]


def forward_kernel(*refs):
    *block_refs, panels_ref, out_ref = refs
    me = lax.axis_index("xl") * 2 + lax.axis_index("core")
    for other, block_ref in enumerate(block_refs):
        product = jnp.dot(block_ref[...], panels_ref[...], preferred_element_type=jnp.float32)
        out_ref[lax.bitwise_xor(me, other)] = product.astype(jnp.bfloat16)


def node_kernel(sums_ref, weight_ref, cotangent_ref, active_ref, out_ref):
    f32, bf16 = jnp.float32, jnp.bfloat16
    members, depth, node_rows, part = sums_ref.shape
    width = members * part
    lanes = out_ref.shape[2]
    share = width // depth
    few = node_rows // 2
    left = lax.broadcasted_iota(jnp.int32, (few, lanes), 1) < share
    sums = [jnp.sum(sums_ref[m].astype(f32), axis=0).astype(bf16) for m in range(members)]
    own_inputs = jnp.concatenate(sums, axis=1)
    pre = jnp.dot(own_inputs, weight_ref[...], preferred_element_type=f32)
    sigma = 1.0 / (1.0 + jnp.exp(-pre))
    active_ref[...] = (pre * sigma).astype(bf16)
    slope = cotangent_ref[...].astype(f32) * (sigma * (1.0 + pre * (1.0 - sigma)))
    slope = slope.astype(bf16)
    proj = lax.dot_general(
        slope, weight_ref[...], (((1,), (1,)), ((), ())), preferred_element_type=f32
    ).astype(bf16)
    packed = []
    for d in range(depth):
        first = d * share // lanes * lanes
        both = own_inputs[:, first : first + lanes].astype(f32)
        early, late = both[:few], both[few:]
        if d * share == first:
            pair = jnp.where(left, early, pltpu.roll(late, share, 1))
        else:
            pair = jnp.where(left, pltpu.roll(early, share, 1), late)
        packed.append(pair.astype(bf16))
    for m in range(members):
        for d in range(depth):
            at = m * depth + d
            out_ref[at, :node_rows] = proj[:, m * part : (m + 1) * part]
            out_ref[at, node_rows : 2 * node_rows] = slope[:, m * part : (m + 1) * part]
            out_ref[at, 2 * node_rows :] = packed[d]


def body(features, weight, cotangent, tile_mask, tile_cols, tile_count, degree):
    f32, bf16 = jnp.float32, jnp.bfloat16
    node_rows, width = features.shape[2], features.shape[3]
    rows = lax.axis_size(ROW)
    depth = lax.axis_size("z")
    cube = lax.axis_size(CUBE)
    part = width // MEMBERS
    col_nodes = rows * node_rows
    block_rows = tile_mask.shape[3]

    vmem, smem = pltpu.VMEM, pltpu.SMEM
    send = local(
        spread_kernel,
        jax.ShapeDtypeStruct((rows // MEMBERS, MEMBERS, node_rows, part), bf16),
        [vmem],
        0,
        2 * col_nodes * part,
        [features[0, 0]],
    )
    panels = lax.all_to_all(send.reshape(rows, node_rows, part), ROW, 0, 0)
    panels = panels.reshape(col_nodes, part)

    slots, tile_width = tile_mask.shape[2], tile_mask.shape[4]
    tiles = local(
        compact_kernel,
        jax.ShapeDtypeStruct((slots * block_rows + 16, tile_width), bf16),
        [smem, smem, vmem, vmem],
        2 * slots * block_rows * tile_width,
        6 * slots * block_rows * tile_width,
        [tile_count[0], tile_cols[0, 0], lax.rsqrt(degree.astype(f32)), tile_mask[0, 0]],
    )
    tiles, core, half = lax.optimization_barrier(
        (tiles, lax.axis_index("core") == 1, lax.axis_index("xl") == 1)
    )
    across = lax.ppermute(tiles, "xl", SWAP)
    blocks = [
        local(
            place_kernel,
            jax.ShapeDtypeStruct((block_rows, col_nodes), bf16),
            [vmem],
            0,
            2 * (slots + 2 * col_nodes // tile_width) * block_rows * tile_width,
            [block],
        )
        for block in (tiles, lax.ppermute(tiles, "core", SWAP), across, lax.ppermute(across, "core", SWAP))
    ]

    partial = local(
        forward_kernel,
        jax.ShapeDtypeStruct((MEMBERS, block_rows, part), bf16),
        [vmem] * (MEMBERS + 1),
        2 * MEMBERS * block_rows * col_nodes * part,
        2 * (MEMBERS * block_rows + part) * col_nodes,
        [*blocks, panels],
    ).reshape(MEMBERS * depth, node_rows, part)
    sums = lax.all_to_all(partial, TEAM, 0, 0).reshape(MEMBERS, depth, node_rows, part)
    share = width // depth
    few = node_rows // 2
    tall = 2 * node_rows + few
    activated, both = local(
        node_kernel,
        (
            jax.ShapeDtypeStruct((node_rows, width), bf16),
            jax.ShapeDtypeStruct((MEMBERS * depth, tall, part), bf16),
        ),
        [vmem, vmem, vmem],
        4 * node_rows * width * width,
        2 * width * width + 8 * col_nodes * part,
        [sums, weight, cotangent[0, 0]],
    )
    both = lax.all_to_all(both, TEAM, 0, 0)
    proj = exclusive(both[:, :node_rows].reshape(MEMBERS, block_rows, part), core, half)
    contract_rows = (((0,), (0,)), ((), ()))
    grad = sum(
        lax.dot_general(b, p, contract_rows, preferred_element_type=f32)
        for b, p in zip(blocks, proj, strict=True)
    )
    grad = grad.astype(bf16).reshape(rows, node_rows, part)
    slope = both[:, node_rows : 2 * node_rows].reshape(-1, 2, few, part)
    slope = jnp.concatenate([slope[:, 0], slope[:, 1]], axis=2).reshape(-1, 2 * part)
    packed = both[:, 2 * node_rows :].reshape(-1, part)
    term = lax.dot_general(packed, slope, contract_rows, preferred_element_type=f32)
    term = term[:share, :part] + term[share:, part:]
    extra = share // cube
    term = term.astype(bf16).reshape(1, 2, 1, MEMBERS, extra, part)
    term = jnp.broadcast_to(term, (rows // (8 * MEMBERS), 2, 4, MEMBERS, extra, part))
    term = term.reshape(rows, extra, part)
    out = lax.all_to_all(jnp.concatenate([grad, term], axis=1), ROW, 0, 0)
    out = out.reshape(rows // MEMBERS, MEMBERS, node_rows + extra, part)
    total = jnp.sum(out[:, :, :node_rows].astype(f32), axis=0)
    feature_grad = jnp.concatenate([total[m] for m in range(MEMBERS)], axis=1).astype(bf16)
    weight_rows = jnp.sum(out[:, :, node_rows:].astype(f32), axis=0)
    weight_rows = jnp.concatenate([weight_rows[m] for m in range(MEMBERS)], axis=1)
    weight_rows, feature_grad = lax.optimization_barrier((weight_rows, feature_grad))
    weight_grad = lax.all_to_all(jnp.broadcast_to(weight_rows[None], (cube, extra, width)), CUBE, 0, 0)
    return (
        activated.reshape(1, 1, node_rows, width),
        feature_grad.reshape(1, 1, node_rows, width),
        weight_grad.reshape(share, width),
    )


def solution(mesh):
    fine = Mesh(mesh.devices.reshape(4, 2, 4, 2, 2, 8), ROW + ("z",))
    in_specs = (
        P("z", ROW, None, None),
        P(),
        P(ROW, "z", None, None),
        P(ROW, "z", None, None, None),
        P(ROW, "z", None),
        P(ROW, "z"),
        P(ROW, None),
    )
    out_specs = (P(ROW, "z", None, None), P("z", ROW, None, None), P("z", None))
    return jax.shard_map(body, mesh=fine, in_specs=in_specs, out_specs=out_specs, check_vma=False)
```
